32 devices in a mesh: ctx: 8 (over z, y), ch: 4 (over x, core).
Axes of the slice: x: 2, y: 2, z: 4, core: 2. Of those that a mesh axis runs over, the one named last changes fastest.
Arguments:
- features: bfloat16 [3, 1024, 8192], P(None, 'ctx', 'ch'), may hold values from -6 to 6
- grad_rows: bfloat16 [1024, 8192], P(('ctx', 'ch')), may hold values from -6 to 6
- conv_taps: float32 [3, 3, 8192], P(None, None, 'ch'), may hold values from -3.5 to 3.5
- decay_rate: float32 [16, 8192], P(None, 'ch'), may hold values from 0 to 1, as said below
- residue: float32 [16, 8192], P(None, 'ch'), may hold values from -1.5 to 1.5
- skip_gain: float32 [8192], P('ch'), may hold values from -1 to 1
Outputs:
- grad_features: bfloat16 [3, 1024, 8192], P(None, 'ctx', 'ch')
The draws below stay inside these ranges and needn't reach their ends.
Inputs may be any that keep to these rules, and one draw needn't show every extreme that they name: `decay_rate`: positive decay rates.
All inputs are finite; a program needn't handle non-finite values.
Results may differ from the reference program's by a relative error of at most 0.00125.
Values may be sent and summed in bfloat16 or wider, within the bound.
A program may use at most 128 MiB of HBM per device.

```python
import math
import jax
import jax.numpy as jnp
from jax import lax

D = 8192
MODES = 16
TAPS = 3
TOKENS = 1024


def draw_decay_rate(key, part):
    key_pick, key_slow, key_fast = jax.random.split(key, 3)
    slow_share = 0.5
    picker = jax.random.uniform(key_pick, (MODES, D), jnp.float32)
    slow_rates = jnp.exp(jax.random.uniform(key_slow, (MODES, D), jnp.float32, math.log(0.2), math.log(16.0))) / TOKENS
    fast_rates = jnp.exp(jax.random.uniform(key_fast, (MODES, D), jnp.float32, math.log(0.001), math.log(0.1)))
    return jnp.where(picker < slow_share, slow_rates, fast_rates).astype(jnp.float32)


def block_scale(rng, extent, cuts, least, top_value):
    loudness = 1.0
    for dim, blocks in cuts:
        steps = jax.random.uniform(jax.random.fold_in(jax.random.fold_in(rng, 6), dim), (blocks,), jnp.float32, least / len(cuts), top_value / len(cuts))
        loudness = loudness * jnp.repeat(jnp.exp(steps), extent[dim] // blocks).reshape((-1,) + (1,) * (len(extent) - 1 - dim))
    return loudness


def noise(stream_key, shape, deviation, reach, cuts=(), held_as=jnp.bfloat16):
    array = deviation * jax.random.normal(stream_key, shape, jnp.float32)
    if cuts:
        array = array * block_scale(stream_key, shape, cuts, -0.22, 0.18)
    return jnp.clip(array, -reach, reach).astype(held_as)


def setup_inputs(seed: int = 0) -> dict:
    keys = jax.random.split(jax.random.key(seed), 7)
    features = noise(keys[0], (3, TOKENS, D), 1.0, 6.0, ((1, 8), (2, 4)))
    grad_rows = noise(keys[1], (TOKENS, D), 1.0, 6.0, ((0, 32),))
    conv_taps = noise(keys[2], (3, TAPS, D), TAPS ** -0.5, 3.5, ((2, 4),), jnp.float32)
    decay_rate = draw_decay_rate(jax.random.fold_in(keys[6], 71), 0)
    residue = noise(keys[4], (MODES, D), MODES ** -0.5, 1.5, ((1, 4),), jnp.float32)
    skip_gain = jnp.clip(jax.random.uniform(keys[5], (D,), jnp.float32, -1.0, 1.0) * block_scale(keys[5], (D,), ((0, 4),), -0.4, 0.0), -1.0, 1.0)
    return {"features": features, "grad_rows": grad_rows, "conv_taps": conv_taps, "decay_rate": decay_rate, "residue": residue, "skip_gain": skip_gain}


def local_pass(signal, decay_rate, gain_in, gain_out):
    total_len, width_dev = signal.shape
    block_len = math.gcd(16, total_len)
    block_count = total_len // block_len
    offsets = jnp.arange(block_len, dtype=jnp.float32)
    rates = decay_rate[None]
    decay_in = jnp.exp(-rates * (block_len - 1.0 - offsets)[:, None, None]) * gain_in[None]
    decay_out = jnp.exp(-rates * (offsets + 1.0)[:, None, None]) * gain_out[None]
    kernel = lax.optimization_barrier(jnp.sum(jnp.exp(-rates * offsets[:, None, None]) * (gain_in * gain_out)[None], axis=1))
    lag_index = jnp.arange(block_len, dtype=jnp.int32)[:, None] - jnp.arange(block_len, dtype=jnp.int32)[None, :]
    toeplitz = jnp.where(lag_index[:, :, None] >= 0, kernel[jnp.maximum(lag_index, 0)], jnp.zeros_like(kernel[:1, None]))
    blocks = signal.reshape(block_count, block_len, width_dev)
    local_out = lax.optimization_barrier(jnp.sum(blocks[:, None, :, :] * toeplitz[None], axis=2))
    block_ends = lax.optimization_barrier(jnp.sum(blocks[:, :, None, :] * decay_in[None], axis=1))
    block_decay = jnp.exp(-decay_rate * block_len)

    def advance(state_now, entry):
        return (block_decay * state_now + entry, state_now)
    final_state, block_starts = lax.scan(advance, jnp.zeros_like(decay_rate), block_ends)
    return (local_out, block_starts, final_state, decay_out)

def finish(pieces, decay_rate, initial):
    local_out, block_starts, final_state, decay_out = pieces
    block_count, block_len, width_dev = local_out.shape
    anchors = jnp.arange(block_count, dtype=jnp.float32) * block_len
    powers = jnp.exp(-decay_rate[None] * anchors[:, None, None])
    states = block_starts + powers * initial[None]
    result = local_out + lax.optimization_barrier(jnp.sum(decay_out[None] * states[:, None], axis=2))
    return result.reshape(block_count * block_len, width_dev)

def causal_taps(signal, tap_weights):
    rim_rows = tap_weights.shape[0] - 1
    total_len = signal.shape[0]
    padded = jnp.pad(signal, ((rim_rows, 0), (0, 0)))
    result = tap_weights[0][None] * padded[rim_rows:rim_rows + total_len]
    for shift_by in range(1, rim_rows + 1):
        result = result + tap_weights[shift_by][None] * padded[rim_rows - shift_by:rim_rows - shift_by + total_len]
    return result

def anticausal_taps(signal, tap_weights):
    rim_rows = tap_weights.shape[0] - 1
    total_len = signal.shape[0]
    padded = jnp.pad(signal, ((0, rim_rows), (0, 0)))
    result = tap_weights[0][None] * padded[0:total_len]
    for shift_by in range(1, rim_rows + 1):
        result = result + tap_weights[shift_by][None] * padded[shift_by:shift_by + total_len]
    return result

def one_group(feats, grad_out, tap_weights, decay_rate, residue, skip_gain):
    signals = feats.astype(jnp.float32)
    queries = causal_taps(signals[0], tap_weights[0])
    keys_feat = causal_taps(signals[1], tap_weights[1])
    values_feat = causal_taps(signals[2], tap_weights[2])
    gain_in = jnp.sqrt(-jnp.expm1(-2.0 * decay_rate))
    product = keys_feat * values_feat
    zero_state = jnp.zeros_like(decay_rate)
    forward = local_pass(product, decay_rate, gain_in, residue)
    conv_out = finish(forward, decay_rate, zero_state) + skip_gain[None] * product
    grad_float = grad_out.astype(jnp.float32)
    grad_query = grad_float * conv_out
    grad_conv = grad_float * queries
    backward = local_pass(grad_conv[::-1], decay_rate, jnp.ones_like(decay_rate), residue * gain_in)
    grad_product = finish(backward, decay_rate, zero_state)[::-1] + skip_gain[None] * grad_conv
    grad_key = grad_product * values_feat
    grad_value = grad_product * keys_feat
    result = jnp.stack([anticausal_taps(grad_query, tap_weights[0]), anticausal_taps(grad_key, tap_weights[1]), anticausal_taps(grad_value, tap_weights[2])])
    return result.astype(jnp.bfloat16)

def reference(features, grad_rows, conv_taps, decay_rate, residue, skip_gain):
    total_len = features.shape[1]
    width_all = features.shape[2]
    tap_count = conv_taps.shape[1]
    mode_count = decay_rate.shape[0]
    group_width = math.gcd(1024, width_all)
    group_count = width_all // group_width
    feats = features.reshape(3, total_len, group_count, group_width).transpose(2, 0, 1, 3)
    grads = grad_rows.reshape(total_len, group_count, group_width).transpose(1, 0, 2)
    tap_groups = conv_taps.reshape(3, tap_count, group_count, group_width).transpose(2, 0, 1, 3)
    rate_groups = decay_rate.reshape(mode_count, group_count, group_width).transpose(1, 0, 2)
    residue_groups = residue.reshape(mode_count, group_count, group_width).transpose(1, 0, 2)
    skip_groups = skip_gain.reshape(group_count, group_width)
    result = lax.map(lambda pieces: one_group(*pieces), (feats, grads, tap_groups, rate_groups, residue_groups, skip_groups))
    return result.transpose(1, 2, 0, 3).reshape(3, total_len, width_all)
```

```python
import functools

import jax
import jax.numpy as jnp
from jax import lax
from jax.experimental import pallas as pl
from jax.experimental.pallas import tpu as pltpu
from jax.sharding import PartitionSpec as P

LANES = 128
SEGS = 8


def one_minus_exp(x):
    series = jnp.ones_like(x)
    for k in range(10, 1, -1):
        series = 1.0 - x * (1.0 / k) * series
    return jnp.where(x < 0.5, x * series, 1.0 - jnp.exp(-x))


def kernel(
    n_ctx,
    n_ch,
    features,
    rows,
    taps,
    rates,
    residue,
    skip,
    out,
    x32,
    grads,
    g32,
    decay,
    seg_decay,
    dev_decay,
    weight,
    short,
    keys,
    values,
    gconv,
    starts,
    partial,
    carry,
    sent,
    landed,
    halo_out,
    halo_in,
    stream,
    rim_out,
    rim_in,
    placed,
    own_sem,
    rows_send,
    rows_recv,
    halo_send,
    halo_recv,
    carry_send,
    carry_recv,
    rim_send,
    rim_recv,
):
    me, mine = lax.axis_index("ctx"), lax.axis_index("ch")
    length, width = features.shape[1], features.shape[2]
    modes = rates.shape[0]
    tiles = width // LANES
    seg = length // SEGS
    piece = rows.shape[0]
    rounds = sent.shape[1]
    group = rim_send.shape[0]
    per = tiles // group

    def lanes(c):
        return pl.ds(pl.multiple_of(c * LANES, LANES), LANES)

    def each(body):
        def step(c, _):
            body(c)
            return 0

        lax.fori_loop(0, tiles, step, 0)

    def wide(row):
        return jnp.broadcast_to(row, (SEGS, LANES))

    place = lax.broadcasted_iota(jnp.int32, (SEGS, LANES), 0)

    barrier = pltpu.get_barrier_semaphore()
    for o in range(1, n_ch):
        pl.semaphore_signal(
            barrier, inc=1, device_id=(me, lax.rem(mine + o, n_ch)), device_id_type=pl.DeviceIdType.MESH
        )
    partners = n_ch - 1
    for k in range(rounds):
        for step in (2**k, -(2**k)):
            there = jnp.logical_and(me + step >= 0, me + step < n_ctx)

            @pl.when(there)
            def _():
                pl.semaphore_signal(
                    barrier, inc=1, device_id=(me + step, mine), device_id_type=pl.DeviceIdType.MESH
                )

            partners = partners + there.astype(jnp.int32)

    def stage(c):
        halo_out[c, 6:8, :] = jnp.zeros((2, LANES), jnp.float32)
        for x in range(3):
            tail = features[x, length - 16 : length, lanes(c)].astype(jnp.float32)
            halo_out[c, 2 * x : 2 * x + 2, :] = tail[14:16]

    each(stage)
    pl.semaphore_wait(barrier, partners)

    halo = pltpu.make_async_remote_copy(
        src_ref=halo_out,
        dst_ref=halo_in,
        send_sem=halo_send,
        recv_sem=halo_recv,
        device_id=(jnp.minimum(me + 1, n_ctx - 1), mine),
        device_id_type=pl.DeviceIdType.MESH,
    )

    @pl.when(me < n_ctx - 1)
    def _():
        halo.start()

    row_copies = []
    spot = pl.ds(pl.multiple_of(mine * piece, piece), piece)
    for o in range(1, n_ch):
        to = lax.rem(mine + o, n_ch)
        row_copies.append(
            pltpu.make_async_remote_copy(
                src_ref=rows.at[:, pl.ds(pl.multiple_of(to * width, LANES), width)],
                dst_ref=grads.at[spot, :],
                send_sem=rows_send.at[o - 1],
                recv_sem=rows_recv.at[o - 1],
                device_id=(me, to),
                device_id_type=pl.DeviceIdType.MESH,
            )
        )
    for copy in row_copies:
        copy.start()
    own = pltpu.make_async_copy(
        rows.at[:, pl.ds(pl.multiple_of(mine * width, LANES), width)], grads.at[spot, :], own_sem
    )
    own.start()

    def prepare(c):
        for x in range(3):
            x32[x, c, 8 : 8 + length, :] = features[x, :, lanes(c)].astype(jnp.float32)
        rate = rates[:, lanes(c)]
        a = jnp.exp(-rate)
        w = residue[:, lanes(c)] * jnp.sqrt(one_minus_exp(2.0 * rate))
        decay[c] = a
        seg_decay[c] = jnp.exp(rate * (-float(seg)))
        dev_decay[c] = jnp.exp(rate * (-float(length)))
        power = w
        for k in range(seg):
            tap = jnp.sum(power, axis=0, keepdims=True)
            if k == 0:
                tap = tap + skip[:, lanes(c)]
            short[c, k : k + 1, :] = tap
            power = power * a
            if k == 0:
                weight[c] = power
        carry[0, c] = jnp.zeros((modes, LANES), jnp.float32)
        carry[1, c] = jnp.zeros((modes, LANES), jnp.float32)

    each(prepare)

    @pl.when(me > 0)
    def _():
        halo.wait_recv()

    @pl.when(me == 0)
    def _():
        halo_in[...] = jnp.zeros(halo_in.shape, jnp.float32)

    def featurized(x, c):
        held = [x32[x, c, pl.ds(8 + j, SEGS, stride=seg), :] for j in range(-2, seg)]
        t = [wide(taps[x, j : j + 1, lanes(c)]) for j in range(3)]
        return [t[0] * held[j + 2] + t[1] * held[j + 1] + t[2] * held[j] for j in range(seg)]

    def ends(signal, c, back):
        order = range(seg - 1, -1, -1) if back else range(seg)
        d = 1 if back else 0
        for low in range(0, modes, 16):
            picked = range(low, min(low + 16, modes))
            a = [wide(decay[c, m : m + 1, :]) for m in picked]
            e = None
            for j in order:
                s = signal[j]
                e = [s] * len(a) if e is None else [a[i] * e[i] + s for i in range(len(a))]
            for i, m in enumerate(picked):
                total = e[i]
                b = wide(seg_decay[c, m : m + 1, :])
                for k in (1, 2, 4):
                    inside = place < SEGS - k if back else place >= k
                    moved = pltpu.roll(total, SEGS - k if back else k, 0)
                    total = total + jnp.where(inside, b, 0.0) * moved
                    b = b * b
                inside = place < SEGS - 1 if back else place >= 1
                moved = pltpu.roll(total, SEGS - 1 if back else 1, 0)
                starts[d, c, m] = jnp.where(inside, moved, 0.0)
                last = total[0:1] if back else total[SEGS - 1 : SEGS]
                sent[d, 0, c, m : m + 1, :] = last

    def reach(d, k):
        return me + 2**k < n_ctx if d == 0 else me >= 2**k

    def comes(d, k):
        return me >= 2**k if d == 0 else me + 2**k < n_ctx

    def carry_copy(d, k):
        to = me + 2**k if d == 0 else me - 2**k
        return pltpu.make_async_remote_copy(
            src_ref=sent.at[d, k],
            dst_ref=landed.at[d, k],
            send_sem=carry_send.at[d, k],
            recv_sem=carry_recv.at[d, k],
            device_id=(jnp.clip(to, 0, n_ctx - 1), mine),
            device_id_type=pl.DeviceIdType.MESH,
        )

    def send(d, k):
        @pl.when(reach(d, k))
        def _():
            carry_copy(d, k).start()

    def take(d, k):
        @pl.when(comes(d, k))
        def _():
            carry_copy(d, k).wait_recv()

            def add(c):
                arrived = landed[d, k, c]
                if k:
                    arrived = arrived * jnp.exp(rates[:, lanes(c)] * (-float(length * (2**k - 1))))
                carry[d, c] = carry[d, c] + arrived

            each(add)

        if k + 1 < rounds:

            @pl.when(reach(d, k + 1))
            def _():
                def join(c):
                    sent[d, k + 1, c] = sent[d, 0, c] + dev_decay[c] * carry[d, c]

                each(join)
                carry_copy(d, k + 1).start()

    def forward_ends(c):
        for x in range(3):
            x32[x, c, 6:8, :] = halo_in[c, 2 * x : 2 * x + 2, :]
        k_now = featurized(1, c)
        v_now = featurized(2, c)
        for j in range(seg):
            keys[c, j] = k_now[j]
            values[c, j] = v_now[j]
        ends([k_now[j] * v_now[j] for j in range(seg)], c, False)

    each(forward_ends)
    if rounds:
        send(0, 0)

    own.wait()
    for copy in row_copies:
        copy.wait()

    def backward_ends(c):
        g32[c] = grads[:, lanes(c)].astype(jnp.float32)
        q_now = featurized(0, c)
        signal = []
        for j in range(seg):
            now = q_now[j] * g32[c, pl.ds(j, SEGS, stride=seg), :]
            gconv[c, j] = now
            signal.append(now)
        ends(signal, c, True)

    each(backward_ends)
    if rounds:
        send(1, 0)
        take(0, 0)

    def forward_short(c):
        h = [wide(short[c, k : k + 1, :]) for k in range(seg)]
        p = [keys[c, j] * values[c, j] for j in range(seg)]
        for j in range(seg):
            total = h[0] * p[j]
            for k in range(1, j + 1):
                total = total + h[k] * p[j - k]
            partial[0, c, j] = total

    each(forward_short)
    if rounds:
        take(1, 0)
    if rounds > 1:
        take(0, 1)

    def backward_short(c):
        h = [wide(short[c, k : k + 1, :]) for k in range(seg)]
        p = [gconv[c, j] for j in range(seg)]
        for j in range(seg):
            total = h[0] * p[j]
            for k in range(1, seg - j):
                total = total + h[k] * p[j + k]
            partial[1, c, j] = total

    each(backward_short)
    if rounds > 1:
        take(1, 1)
    for k in range(2, rounds):
        take(0, k)
        if k + 1 < rounds:
            take(1, k)

    def complete(c, d):
        a = [wide(decay[c, m : m + 1, :]) for m in range(modes)]
        y = []
        count = (SEGS - 1 - place if d else place).astype(jnp.float32) * (-float(seg))
        for m in range(modes):
            entering = jnp.exp(wide(rates[m : m + 1, lanes(c)]) * count)
            state = starts[d, c, m] + entering * wide(carry[d, c, m : m + 1, :])
            y.append(wide(weight[c, m : m + 1, :]) * state)
        result = [None] * seg
        order = range(seg - 1, -1, -1) if d else range(seg)
        for step, j in enumerate(order):
            total = partial[d, c, j]
            if step:
                y = [y[m] * a[m] for m in range(modes)]
            for m in range(modes):
                total = total + y[m]
            result[j] = total
        return result

    def forward_finish(c):
        conv = complete(c, 0)
        for j in range(seg):
            stream[0, c, j] = conv[j] * g32[c, pl.ds(j, SEGS, stride=seg), :]

    each(forward_finish)
    if rounds > 2:
        take(1, rounds - 1)

    def rim_copy(g):
        some = pl.ds(g * per, per)
        return pltpu.make_async_remote_copy(
            src_ref=rim_out.at[some],
            dst_ref=rim_in.at[some],
            send_sem=rim_send.at[g],
            recv_sem=rim_recv.at[g],
            device_id=(jnp.maximum(me - 1, 0), mine),
            device_id_type=pl.DeviceIdType.MESH,
        )

    def backward_finish(c):
        prod = complete(c, 1)
        for j in range(seg):
            stream[1, c, j] = prod[j] * values[c, j]
            stream[2, c, j] = prod[j] * keys[c, j]
        rim_out[c, 6:8, :] = jnp.zeros((2, LANES), jnp.float32)
        for x in range(3):
            for r in range(2):
                rim_out[c, 2 * x + r : 2 * x + r + 1, :] = stream[x, c, r, 0:1, :]

    def finish_group(g, _):
        def one(i, _):
            backward_finish(g * per + i)
            return 0

        lax.fori_loop(0, per, one, 0)

        @pl.when(me > 0)
        def _():
            rim_copy(g).start()

        return 0

    lax.fori_loop(0, group, finish_group, 0)

    @pl.when(me == n_ctx - 1)
    def _():
        rim_in[...] = jnp.zeros(rim_in.shape, jnp.float32)

    def last_taps(c):
        for x in range(3):
            t = [wide(taps[x, j : j + 1, lanes(c)]) for j in range(3)]
            g = [stream[x, c, j] for j in range(seg)]
            for r in range(2):
                moved = pltpu.roll(g[r], SEGS - 1, 0)
                g.append(jnp.where(place == SEGS - 1, wide(rim_in[c, 2 * x + r : 2 * x + r + 1, :]), moved))
            for j in range(seg):
                placed[x, pl.ds(j, SEGS, stride=seg), :] = t[0] * g[j] + t[1] * g[j + 1] + t[2] * g[j + 2]
            out[x, :, lanes(c)] = placed[x].astype(out.dtype)

    def output_group(g, _):
        @pl.when(me < n_ctx - 1)
        def _():
            rim_copy(g).wait_recv()

        def one(i, _):
            last_taps(g * per + i)
            return 0

        lax.fori_loop(0, per, one, 0)
        return 0

    lax.fori_loop(0, group, output_group, 0)

    @pl.when(me < n_ctx - 1)
    def _():
        halo.wait_send()

    for d in range(2):
        for k in range(rounds):

            @pl.when(reach(d, k))
            def _():
                carry_copy(d, k).wait_send()

    @pl.when(me > 0)
    def _():
        def drain(g, _):
            rim_copy(g).wait_send()
            return 0

        lax.fori_loop(0, group, drain, 0)


def per_device(n_ctx, n_ch, features, grad_rows, conv_taps, decay_rate, residue, skip_gain):
    _, length, width = features.shape
    modes = decay_rate.shape[0]
    tiles = width // LANES
    seg = length // SEGS
    rounds = (n_ctx - 1).bit_length()
    group = 4 if tiles % 4 == 0 else 1
    f32 = jnp.float32
    dma = pltpu.SemaphoreType.DMA
    vmem = pl.BlockSpec(memory_space=pltpu.VMEM)
    table = pltpu.VMEM((tiles, modes, LANES), f32)
    tokens = pltpu.VMEM((tiles, seg, SEGS, LANES), f32)
    edge = pltpu.VMEM((tiles, 8, LANES), f32)
    return pl.pallas_call(
        functools.partial(kernel, n_ctx, n_ch),
        out_shape=jax.ShapeDtypeStruct(features.shape, jnp.bfloat16),
        in_specs=[vmem] * 6,
        out_specs=vmem,
        scratch_shapes=[
            pltpu.VMEM((3, tiles, 8 + length, LANES), f32),
            pltpu.VMEM((length, width), jnp.bfloat16),
            pltpu.VMEM((tiles, length, LANES), f32),
            table,
            table,
            table,
            table,
            pltpu.VMEM((tiles, seg, LANES), f32),
            tokens,
            tokens,
            tokens,
            pltpu.VMEM((2, tiles, modes, SEGS, LANES), f32),
            pltpu.VMEM((2, tiles, seg, SEGS, LANES), f32),
            pltpu.VMEM((2, tiles, modes, LANES), f32),
            pltpu.VMEM((2, rounds, tiles, modes, LANES), f32),
            pltpu.VMEM((2, rounds, tiles, modes, LANES), f32),
            edge,
            edge,
            pltpu.VMEM((3, tiles, seg, SEGS, LANES), f32),
            edge,
            edge,
            pltpu.VMEM((3, length, LANES), f32),
            dma,
            dma((n_ch - 1,)),
            dma((n_ch - 1,)),
            dma,
            dma,
            dma((2, rounds)),
            dma((2, rounds)),
            dma((group,)),
            dma((group,)),
        ],
        compiler_params=pltpu.CompilerParams(
            collective_id=0, has_side_effects=True, vmem_limit_bytes=48 * 1024 * 1024
        ),
    )(features, grad_rows, conv_taps, decay_rate, residue, skip_gain[None])


def solution(mesh):
    in_specs = (
        P(None, "ctx", "ch"),
        P(("ctx", "ch"), None),
        P(None, None, "ch"),
        P(None, "ch"),
        P(None, "ch"),
        P("ch"),
    )
    body = functools.partial(per_device, mesh.shape["ctx"], mesh.shape["ch"])
    return jax.shard_map(
        body, mesh=mesh, in_specs=in_specs, out_specs=P(None, "ctx", "ch"), check_vma=False
    )
```

```python
import functools

import jax
import jax.numpy as jnp
from jax import lax
from jax.experimental import pallas as pl
from jax.experimental.pallas import tpu as pltpu
from jax.sharding import PartitionSpec as P

LANES = 128
SEGS = 8


def one_minus_exp(x):
    series = jnp.ones_like(x)
    for k in range(10, 1, -1):
        series = 1.0 - x * (1.0 / k) * series
    return jnp.where(x < 0.5, x * series, 1.0 - jnp.exp(-x))


def kernel(
    n_ctx,
    n_ch,
    features_hbm,
    rows,
    taps_hbm,
    rates_hbm,
    residue_hbm,
    skip_hbm,
    out,
    features,
    taps,
    rates,
    residue,
    skip,
    x32,
    grads,
    g32,
    decay,
    seg_decay,
    dev_decay,
    weight,
    short,
    keys,
    values,
    gconv,
    starts,
    partial,
    carry,
    sent,
    landed,
    halo_out,
    halo_in,
    stream,
    rim_out,
    rim_in,
    placed,
    load_sem,
    own_sem,
    rows_send,
    rows_recv,
    halo_send,
    halo_recv,
    carry_send,
    carry_recv,
    rim_send,
    rim_recv,
):
    me, mine = lax.axis_index("ctx"), lax.axis_index("ch")
    length, width = features.shape[1], features.shape[2]
    modes = rates.shape[0]
    tiles = width // LANES
    seg = length // SEGS
    piece = rows.shape[0]
    rounds = sent.shape[1]
    group = rim_send.shape[0]
    per = tiles // group

    def lanes(c):
        return pl.ds(pl.multiple_of(c * LANES, LANES), LANES)

    def loop(count, body, first=0):
        def step(i, _):
            body(first + i)
            return 0

        lax.fori_loop(0, count, step, 0)

    def each(body):
        loop(tiles, body)

    def within(g, body):
        loop(per, body, g * per)

    def wide(row):
        return jnp.broadcast_to(row, (SEGS, LANES))

    place = lax.broadcasted_iota(jnp.int32, (SEGS, LANES), 0)

    loads = [
        pltpu.make_async_copy(far, near, load_sem.at[i])
        for i, (far, near) in enumerate(
            (
                (features_hbm, features),
                (rates_hbm, rates),
                (taps_hbm, taps),
                (residue_hbm, residue),
                (skip_hbm, skip),
            )
        )
    ]
    for load in loads:
        load.start()

    barrier = pltpu.get_barrier_semaphore()
    for o in range(1, n_ch):
        pl.semaphore_signal(
            barrier, inc=1, device_id=(me, lax.rem(mine + o, n_ch)), device_id_type=pl.DeviceIdType.MESH
        )
    partners = n_ch - 1
    for k in range(rounds):
        for step in (2**k, -(2**k)):
            there = jnp.logical_and(me + step >= 0, me + step < n_ctx)

            @pl.when(there)
            def _():
                pl.semaphore_signal(
                    barrier, inc=1, device_id=(me + step, mine), device_id_type=pl.DeviceIdType.MESH
                )

            partners = partners + there.astype(jnp.int32)

    pl.semaphore_wait(barrier, partners)

    row_copies = []
    spot = pl.ds(pl.multiple_of(mine * piece, piece), piece)
    for o in range(1, n_ch):
        to = lax.rem(mine + o, n_ch)
        row_copies.append(
            pltpu.make_async_remote_copy(
                src_ref=rows.at[:, pl.ds(pl.multiple_of(to * width, LANES), width)],
                dst_ref=grads.at[spot, :],
                send_sem=rows_send.at[o - 1],
                recv_sem=rows_recv.at[o - 1],
                device_id=(me, to),
                device_id_type=pl.DeviceIdType.MESH,
            )
        )
    for copy in row_copies:
        copy.start()
    own = pltpu.make_async_copy(
        rows.at[:, pl.ds(pl.multiple_of(mine * width, LANES), width)], grads.at[spot, :], own_sem
    )
    own.start()

    def stage(c):
        halo_out[c, 6:8, :] = jnp.zeros((2, LANES), jnp.float32)
        for x in range(3):
            tail = features[x, length - 16 : length, lanes(c)].astype(jnp.float32)
            halo_out[c, 2 * x : 2 * x + 2, :] = tail[14:16]

    loads[0].wait()
    each(stage)

    halo = pltpu.make_async_remote_copy(
        src_ref=halo_out,
        dst_ref=halo_in,
        send_sem=halo_send,
        recv_sem=halo_recv,
        device_id=(jnp.minimum(me + 1, n_ctx - 1), mine),
        device_id_type=pl.DeviceIdType.MESH,
    )

    @pl.when(me < n_ctx - 1)
    def _():
        halo.start()

    def prepare(c):
        for x in range(3):
            x32[x, c, 8 : 8 + length, :] = features[x, :, lanes(c)].astype(jnp.float32)
        rate = rates[:, lanes(c)]
        decay[c] = jnp.exp(-rate)
        seg_decay[c] = jnp.exp(rate * (-float(seg)))
        dev_decay[c] = jnp.exp(rate * (-float(length)))
        carry[0, c] = jnp.zeros((modes, LANES), jnp.float32)
        carry[1, c] = jnp.zeros((modes, LANES), jnp.float32)

    def filters(c):
        a = decay[c]
        power = residue[:, lanes(c)] * jnp.sqrt(one_minus_exp(2.0 * rates[:, lanes(c)]))
        for k in range(seg):
            tap = jnp.sum(power, axis=0, keepdims=True)
            if k == 0:
                tap = tap + skip[:, lanes(c)]
            short[c, k : k + 1, :] = tap
            power = power * a
            if k == 0:
                weight[c] = power

    loads[1].wait()
    each(prepare)
    loads[2].wait()

    @pl.when(me > 0)
    def _():
        halo.wait_recv()

    @pl.when(me == 0)
    def _():
        halo_in[...] = jnp.zeros(halo_in.shape, jnp.float32)

    def featurized(x, c):
        held = [x32[x, c, pl.ds(8 + j, SEGS, stride=seg), :] for j in range(-2, seg)]
        t = [wide(taps[x, j : j + 1, lanes(c)]) for j in range(3)]
        return [t[0] * held[j + 2] + t[1] * held[j + 1] + t[2] * held[j] for j in range(seg)]

    def ends(signal, c, back):
        order = range(seg - 1, -1, -1) if back else range(seg)
        d = 1 if back else 0
        for low in range(0, modes, 16):
            picked = range(low, min(low + 16, modes))
            a = [wide(decay[c, m : m + 1, :]) for m in picked]
            e = None
            for j in order:
                s = signal[j]
                e = [s] * len(a) if e is None else [a[i] * e[i] + s for i in range(len(a))]
            for i, m in enumerate(picked):
                total = e[i]
                b = wide(seg_decay[c, m : m + 1, :])
                for k in (1, 2, 4):
                    inside = place < SEGS - k if back else place >= k
                    moved = pltpu.roll(total, SEGS - k if back else k, 0)
                    total = total + jnp.where(inside, b, 0.0) * moved
                    b = b * b
                inside = place < SEGS - 1 if back else place >= 1
                moved = pltpu.roll(total, SEGS - 1 if back else 1, 0)
                starts[d, c, m] = jnp.where(inside, moved, 0.0)
                last = total[0:1] if back else total[SEGS - 1 : SEGS]
                sent[d, 0, c, m : m + 1, :] = last

    def reach(d, k):
        return me + 2**k < n_ctx if d == 0 else me >= 2**k

    def comes(d, k):
        return me >= 2**k if d == 0 else me + 2**k < n_ctx

    def carry_copy(d, k, g):
        some = pl.ds(g * per, per)
        to = me + 2**k if d == 0 else me - 2**k
        return pltpu.make_async_remote_copy(
            src_ref=sent.at[d, k, some],
            dst_ref=landed.at[d, k, some],
            send_sem=carry_send.at[d, k, g],
            recv_sem=carry_recv.at[d, k, g],
            device_id=(jnp.clip(to, 0, n_ctx - 1), mine),
            device_id_type=pl.DeviceIdType.MESH,
        )

    def send(d, k, g):
        @pl.when(reach(d, k))
        def _():
            carry_copy(d, k, g).start()

    def take(d, k, g):
        @pl.when(comes(d, k))
        def _():
            carry_copy(d, k, g).wait_recv()

            def add(c):
                arrived = landed[d, k, c]
                if k:
                    arrived = arrived * jnp.exp(rates[:, lanes(c)] * (-float(length * (2**k - 1))))
                carry[d, c] = carry[d, c] + arrived

            within(g, add)

        if k + 1 < rounds:

            @pl.when(reach(d, k + 1))
            def _():
                def join(c):
                    sent[d, k + 1, c] = sent[d, 0, c] + dev_decay[c] * carry[d, c]

                within(g, join)
                carry_copy(d, k + 1, g).start()

    def forward_ends(c):
        for x in range(3):
            x32[x, c, 6:8, :] = halo_in[c, 2 * x : 2 * x + 2, :]
        k_now = featurized(1, c)
        v_now = featurized(2, c)
        for j in range(seg):
            keys[c, j] = k_now[j]
            values[c, j] = v_now[j]
        ends([k_now[j] * v_now[j] for j in range(seg)], c, False)

    def forward_ends_group(g):
        within(g, forward_ends)
        if rounds:
            send(0, 0, g)

    loop(group, forward_ends_group)
    loads[3].wait()
    loads[4].wait()
    each(filters)

    own.wait()
    for copy in row_copies:
        copy.wait()

    def backward_ends(c):
        g32[c] = grads[:, lanes(c)].astype(jnp.float32)
        q_now = featurized(0, c)
        signal = []
        for j in range(seg):
            now = q_now[j] * g32[c, pl.ds(j, SEGS, stride=seg), :]
            gconv[c, j] = now
            signal.append(now)
        ends(signal, c, True)

    def backward_ends_group(g):
        within(g, backward_ends)
        if rounds:
            send(1, 0, g)
            take(0, 0, g)

    loop(group, backward_ends_group)

    def forward_short(c):
        h = [wide(short[c, k : k + 1, :]) for k in range(seg)]
        p = [keys[c, j] * values[c, j] for j in range(seg)]
        for j in range(seg):
            total = h[0] * p[j]
            for k in range(1, j + 1):
                total = total + h[k] * p[j - k]
            partial[0, c, j] = total

    def forward_short_group(g):
        within(g, forward_short)
        if rounds:
            take(1, 0, g)
        if rounds > 1:
            take(0, 1, g)

    loop(group, forward_short_group)

    def backward_short(c):
        h = [wide(short[c, k : k + 1, :]) for k in range(seg)]
        p = [gconv[c, j] for j in range(seg)]
        for j in range(seg):
            total = h[0] * p[j]
            for k in range(1, seg - j):
                total = total + h[k] * p[j + k]
            partial[1, c, j] = total

    def backward_short_group(g):
        within(g, backward_short)
        if rounds > 1:
            take(1, 1, g)

    loop(group, backward_short_group)
    for k in range(2, rounds - 1):

        def both(g):
            take(0, k, g)
            take(1, k, g)

        loop(group, both)

    def complete(c, d):
        a = [wide(decay[c, m : m + 1, :]) for m in range(modes)]
        y = []
        count = (SEGS - 1 - place if d else place).astype(jnp.float32) * (-float(seg))
        for m in range(modes):
            entering = jnp.exp(wide(rates[m : m + 1, lanes(c)]) * count)
            state = starts[d, c, m] + entering * wide(carry[d, c, m : m + 1, :])
            y.append(wide(weight[c, m : m + 1, :]) * state)
        result = [None] * seg
        order = range(seg - 1, -1, -1) if d else range(seg)
        for step, j in enumerate(order):
            total = partial[d, c, j]
            if step:
                y = [y[m] * a[m] for m in range(modes)]
            for m in range(modes):
                total = total + y[m]
            result[j] = total
        return result

    def forward_finish(c):
        conv = complete(c, 0)
        for j in range(seg):
            stream[0, c, j] = conv[j] * g32[c, pl.ds(j, SEGS, stride=seg), :]

    def forward_finish_group(g):
        if rounds > 2:
            take(0, rounds - 1, g)
        within(g, forward_finish)

    loop(group, forward_finish_group)

    def rim_copy(g):
        some = pl.ds(g * per, per)
        return pltpu.make_async_remote_copy(
            src_ref=rim_out.at[some],
            dst_ref=rim_in.at[some],
            send_sem=rim_send.at[g],
            recv_sem=rim_recv.at[g],
            device_id=(jnp.maximum(me - 1, 0), mine),
            device_id_type=pl.DeviceIdType.MESH,
        )

    def backward_finish(c):
        prod = complete(c, 1)
        for j in range(seg):
            stream[1, c, j] = prod[j] * values[c, j]
            stream[2, c, j] = prod[j] * keys[c, j]
        rim_out[c, 6:8, :] = jnp.zeros((2, LANES), jnp.float32)
        for x in range(3):
            for r in range(2):
                rim_out[c, 2 * x + r : 2 * x + r + 1, :] = stream[x, c, r, 0:1, :]

    def backward_finish_group(g):
        if rounds > 2:
            take(1, rounds - 1, g)
        within(g, backward_finish)

        @pl.when(me > 0)
        def _():
            rim_copy(g).start()

    loop(group, backward_finish_group)

    @pl.when(me == n_ctx - 1)
    def _():
        rim_in[...] = jnp.zeros(rim_in.shape, jnp.float32)

    def last_taps(c):
        for x in range(3):
            t = [wide(taps[x, j : j + 1, lanes(c)]) for j in range(3)]
            g = [stream[x, c, j] for j in range(seg)]
            for r in range(2):
                moved = pltpu.roll(g[r], SEGS - 1, 0)
                g.append(jnp.where(place == SEGS - 1, wide(rim_in[c, 2 * x + r : 2 * x + r + 1, :]), moved))
            for j in range(seg):
                placed[x, pl.ds(j, SEGS, stride=seg), :] = t[0] * g[j] + t[1] * g[j + 1] + t[2] * g[j + 2]
            out[x, :, lanes(c)] = placed[x].astype(out.dtype)

    def output_group(g):
        @pl.when(me < n_ctx - 1)
        def _():
            rim_copy(g).wait_recv()

        within(g, last_taps)

    loop(group, output_group)

    @pl.when(me < n_ctx - 1)
    def _():
        halo.wait_send()

    for d in range(2):
        for k in range(rounds):

            @pl.when(reach(d, k))
            def _():
                loop(group, lambda g: carry_copy(d, k, g).wait_send())

    @pl.when(me > 0)
    def _():
        loop(group, lambda g: rim_copy(g).wait_send())


def per_device(n_ctx, n_ch, features, grad_rows, conv_taps, decay_rate, residue, skip_gain):
    _, length, width = features.shape
    modes = decay_rate.shape[0]
    tiles = width // LANES
    seg = length // SEGS
    rounds = (n_ctx - 1).bit_length()
    group = 4 if tiles % 4 == 0 else 1
    f32 = jnp.float32
    dma = pltpu.SemaphoreType.DMA
    vmem = pl.BlockSpec(memory_space=pltpu.VMEM)
    table = pltpu.VMEM((tiles, modes, LANES), f32)
    tokens = pltpu.VMEM((tiles, seg, SEGS, LANES), f32)
    edge = pltpu.VMEM((tiles, 8, LANES), f32)
    return pl.pallas_call(
        functools.partial(kernel, n_ctx, n_ch),
        out_shape=jax.ShapeDtypeStruct(features.shape, jnp.bfloat16),
        in_specs=[pl.BlockSpec(memory_space=pl.ANY)] * 6,
        out_specs=vmem,
        scratch_shapes=[
            pltpu.VMEM(features.shape, features.dtype),
            pltpu.VMEM(conv_taps.shape, f32),
            pltpu.VMEM(decay_rate.shape, f32),
            pltpu.VMEM(residue.shape, f32),
            pltpu.VMEM((1, width), f32),
            pltpu.VMEM((3, tiles, 8 + length, LANES), f32),
            pltpu.VMEM((length, width), jnp.bfloat16),
            pltpu.VMEM((tiles, length, LANES), f32),
            table,
            table,
            table,
            table,
            pltpu.VMEM((tiles, seg, LANES), f32),
            tokens,
            tokens,
            tokens,
            pltpu.VMEM((2, tiles, modes, SEGS, LANES), f32),
            pltpu.VMEM((2, tiles, seg, SEGS, LANES), f32),
            pltpu.VMEM((2, tiles, modes, LANES), f32),
            pltpu.VMEM((2, rounds, tiles, modes, LANES), f32),
            pltpu.VMEM((2, rounds, tiles, modes, LANES), f32),
            edge,
            edge,
            pltpu.VMEM((3, tiles, seg, SEGS, LANES), f32),
            edge,
            edge,
            pltpu.VMEM((3, length, LANES), f32),
            dma((5,)),
            dma,
            dma((n_ch - 1,)),
            dma((n_ch - 1,)),
            dma,
            dma,
            dma((2, rounds, group)),
            dma((2, rounds, group)),
            dma((group,)),
            dma((group,)),
        ],
        compiler_params=pltpu.CompilerParams(
            collective_id=0, has_side_effects=True, vmem_limit_bytes=56 * 1024 * 1024
        ),
    )(features, grad_rows, conv_taps, decay_rate, residue, skip_gain[None])


def solution(mesh):
    in_specs = (
        P(None, "ctx", "ch"),
        P(("ctx", "ch"), None),
        P(None, None, "ch"),
        P(None, "ch"),
        P(None, "ch"),
        P("ch"),
    )
    body = functools.partial(per_device, mesh.shape["ctx"], mesh.shape["ch"])
    return jax.shard_map(
        body, mesh=mesh, in_specs=in_specs, out_specs=P(None, "ctx", "ch"), check_vma=False
    )
```

```python
import functools

import jax
import jax.numpy as jnp
from jax import lax
from jax.experimental import pallas as pl
from jax.experimental.pallas import tpu as pltpu
from jax.sharding import PartitionSpec as P

LANES = 128
SEGS = 8


def one_minus_exp(x):
    series = jnp.ones_like(x)
    for k in range(10, 1, -1):
        series = 1.0 - x * (1.0 / k) * series
    return jnp.where(x < 0.5, x * series, 1.0 - jnp.exp(-x))


def added(terms):
    sums = list(terms[:4])
    for i, term in enumerate(terms[4:]):
        sums[i % 4] = sums[i % 4] + term
    while len(sums) > 1:
        sums = [sums[i] + sums[i + 1] if i + 1 < len(sums) else sums[i] for i in range(0, len(sums), 2)]
    return sums[0]


def kernel(
    n_ctx,
    n_ch,
    features_hbm,
    rows,
    taps_hbm,
    rates_hbm,
    residue_hbm,
    skip_hbm,
    out,
    features,
    taps,
    rates,
    residue,
    skip,
    x32,
    grads,
    g32,
    decay,
    seg_decay,
    dev_decay,
    weight,
    short,
    keys,
    values,
    gconv,
    starts,
    partial,
    carry,
    sent,
    landed,
    halo_out,
    halo_in,
    stream,
    rim_out,
    rim_in,
    placed,
    load_sem,
    own_sem,
    rows_send,
    rows_recv,
    halo_send,
    halo_recv,
    carry_send,
    carry_recv,
    rim_send,
    rim_recv,
):
    me, mine = lax.axis_index("ctx"), lax.axis_index("ch")
    length, width = features.shape[1], features.shape[2]
    modes = rates.shape[0]
    tiles = width // LANES
    seg = length // SEGS
    piece = rows.shape[0]
    rounds = sent.shape[1]
    group = rim_send.shape[0]
    per = tiles // group

    def lanes(c):
        return pl.ds(pl.multiple_of(c * LANES, LANES), LANES)

    def loop(count, body, first=0):
        def step(i, _):
            body(first + i)
            return 0

        lax.fori_loop(0, count, step, 0)

    def each(body):
        loop(tiles, body)

    def within(g, body):
        loop(per, body, g * per)

    def wide(row):
        return jnp.broadcast_to(row, (SEGS, LANES))

    place = lax.broadcasted_iota(jnp.int32, (SEGS, LANES), 0)

    loads = [
        pltpu.make_async_copy(far, near, load_sem.at[i])
        for i, (far, near) in enumerate(
            (
                (features_hbm, features),
                (rates_hbm, rates),
                (taps_hbm, taps),
                (residue_hbm, residue),
                (skip_hbm, skip),
            )
        )
    ]
    for load in loads:
        load.start()

    barrier = pltpu.get_barrier_semaphore()
    for o in range(1, n_ch):
        pl.semaphore_signal(
            barrier, inc=1, device_id=(me, lax.rem(mine + o, n_ch)), device_id_type=pl.DeviceIdType.MESH
        )
    partners = n_ch - 1
    for k in range(rounds):
        for step in (2**k, -(2**k)):
            there = jnp.logical_and(me + step >= 0, me + step < n_ctx)

            @pl.when(there)
            def _():
                pl.semaphore_signal(
                    barrier, inc=1, device_id=(me + step, mine), device_id_type=pl.DeviceIdType.MESH
                )

            partners = partners + there.astype(jnp.int32)

    pl.semaphore_wait(barrier, partners)

    row_copies = []
    spot = pl.ds(pl.multiple_of(mine * piece, piece), piece)
    for o in range(1, n_ch):
        to = lax.rem(mine + o, n_ch)
        row_copies.append(
            pltpu.make_async_remote_copy(
                src_ref=rows.at[:, pl.ds(pl.multiple_of(to * width, LANES), width)],
                dst_ref=grads.at[spot, :],
                send_sem=rows_send.at[o - 1],
                recv_sem=rows_recv.at[o - 1],
                device_id=(me, to),
                device_id_type=pl.DeviceIdType.MESH,
            )
        )
    for copy in row_copies:
        copy.start()
    own = pltpu.make_async_copy(
        rows.at[:, pl.ds(pl.multiple_of(mine * width, LANES), width)], grads.at[spot, :], own_sem
    )
    own.start()

    def stage(c):
        halo_out[c, 6:8, :] = jnp.zeros((2, LANES), jnp.float32)
        for x in range(3):
            tail = features[x, length - 16 : length, lanes(c)].astype(jnp.float32)
            halo_out[c, 2 * x : 2 * x + 2, :] = tail[14:16]

    loads[0].wait()
    each(stage)

    halo = pltpu.make_async_remote_copy(
        src_ref=halo_out,
        dst_ref=halo_in,
        send_sem=halo_send,
        recv_sem=halo_recv,
        device_id=(jnp.minimum(me + 1, n_ctx - 1), mine),
        device_id_type=pl.DeviceIdType.MESH,
    )

    @pl.when(me < n_ctx - 1)
    def _():
        halo.start()

    def prepare(c):
        for x in range(3):
            x32[x, c, 8 : 8 + length, :] = features[x, :, lanes(c)].astype(jnp.float32)
        rate = rates[:, lanes(c)]
        decay[c] = jnp.exp(-rate)
        seg_decay[c] = jnp.exp(rate * (-float(seg)))
        dev_decay[c] = jnp.exp(rate * (-float(length)))
        carry[0, c] = jnp.zeros((modes, LANES), jnp.float32)
        carry[1, c] = jnp.zeros((modes, LANES), jnp.float32)

    def filters(c):
        a = decay[c]
        power = residue[:, lanes(c)] * jnp.sqrt(one_minus_exp(2.0 * rates[:, lanes(c)]))
        for k in range(seg):
            tap = jnp.sum(power, axis=0, keepdims=True)
            if k == 0:
                tap = tap + skip[:, lanes(c)]
            short[c, k : k + 1, :] = tap
            power = power * a
            if k == 0:
                weight[c] = power

    loads[1].wait()
    each(prepare)
    loads[2].wait()

    @pl.when(me > 0)
    def _():
        halo.wait_recv()

    @pl.when(me == 0)
    def _():
        halo_in[...] = jnp.zeros(halo_in.shape, jnp.float32)

    def featurized(x, c):
        held = [x32[x, c, pl.ds(8 + j, SEGS, stride=seg), :] for j in range(-2, seg)]
        t = [wide(taps[x, j : j + 1, lanes(c)]) for j in range(3)]
        return [t[0] * held[j + 2] + t[1] * held[j + 1] + t[2] * held[j] for j in range(seg)]

    def ends(signal, c, back):
        order = range(seg - 1, -1, -1) if back else range(seg)
        d = 1 if back else 0
        for low in range(0, modes, 16):
            picked = range(low, min(low + 16, modes))
            a = [wide(decay[c, m : m + 1, :]) for m in picked]
            e = None
            for j in order:
                s = signal[j]
                e = [s] * len(a) if e is None else [a[i] * e[i] + s for i in range(len(a))]
            for i, m in enumerate(picked):
                total = e[i]
                b = wide(seg_decay[c, m : m + 1, :])
                for k in (1, 2, 4):
                    inside = place < SEGS - k if back else place >= k
                    moved = pltpu.roll(total, SEGS - k if back else k, 0)
                    total = total + jnp.where(inside, b, 0.0) * moved
                    b = b * b
                inside = place < SEGS - 1 if back else place >= 1
                moved = pltpu.roll(total, SEGS - 1 if back else 1, 0)
                starts[d, c, m] = jnp.where(inside, moved, 0.0)
                last = total[0:1] if back else total[SEGS - 1 : SEGS]
                sent[d, 0, c, m : m + 1, :] = last

    def reach(d, k):
        return me + 2**k < n_ctx if d == 0 else me >= 2**k

    def comes(d, k):
        return me >= 2**k if d == 0 else me + 2**k < n_ctx

    def carry_copy(d, k, g):
        some = pl.ds(g * per, per)
        to = me + 2**k if d == 0 else me - 2**k
        return pltpu.make_async_remote_copy(
            src_ref=sent.at[d, k, some],
            dst_ref=landed.at[d, k, some],
            send_sem=carry_send.at[d, k, g],
            recv_sem=carry_recv.at[d, k, g],
            device_id=(jnp.clip(to, 0, n_ctx - 1), mine),
            device_id_type=pl.DeviceIdType.MESH,
        )

    def send(d, k, g):
        @pl.when(reach(d, k))
        def _():
            carry_copy(d, k, g).start()

    def take(d, k, g):
        @pl.when(comes(d, k))
        def _():
            carry_copy(d, k, g).wait_recv()

            def add(c):
                arrived = landed[d, k, c]
                if k:
                    arrived = arrived * jnp.exp(rates[:, lanes(c)] * (-float(length * (2**k - 1))))
                carry[d, c] = carry[d, c] + arrived

            within(g, add)

        if k + 1 < rounds:

            @pl.when(reach(d, k + 1))
            def _():
                def join(c):
                    sent[d, k + 1, c] = sent[d, 0, c] + dev_decay[c] * carry[d, c]

                within(g, join)
                carry_copy(d, k + 1, g).start()

    def forward_ends(c):
        for x in range(3):
            x32[x, c, 6:8, :] = halo_in[c, 2 * x : 2 * x + 2, :]
        k_now = featurized(1, c)
        v_now = featurized(2, c)
        for j in range(seg):
            keys[c, j] = k_now[j]
            values[c, j] = v_now[j]
        ends([k_now[j] * v_now[j] for j in range(seg)], c, False)

    def forward_ends_group(g):
        within(g, forward_ends)
        if rounds:
            send(0, 0, g)

    loop(group, forward_ends_group)
    loads[3].wait()
    loads[4].wait()
    each(filters)

    own.wait()
    for copy in row_copies:
        copy.wait()

    def backward_ends(c):
        g32[c] = grads[:, lanes(c)].astype(jnp.float32)
        q_now = featurized(0, c)
        signal = []
        for j in range(seg):
            now = q_now[j] * g32[c, pl.ds(j, SEGS, stride=seg), :]
            gconv[c, j] = now
            signal.append(now)
        ends(signal, c, True)

    def backward_ends_group(g):
        within(g, backward_ends)
        if rounds:
            send(1, 0, g)
            take(0, 0, g)

    loop(group, backward_ends_group)

    def forward_short(c):
        h = [wide(short[c, k : k + 1, :]) for k in range(seg)]
        p = [keys[c, j] * values[c, j] for j in range(seg)]
        for j in range(seg):
            partial[0, c, j] = added([h[k] * p[j - k] for k in range(j + 1)])

    def forward_short_group(g):
        within(g, forward_short)
        if rounds:
            take(1, 0, g)
        if rounds > 1:
            take(0, 1, g)

    loop(group, forward_short_group)

    def backward_short(c):
        h = [wide(short[c, k : k + 1, :]) for k in range(seg)]
        p = [gconv[c, j] for j in range(seg)]
        for j in range(seg):
            partial[1, c, j] = added([h[k] * p[j + k] for k in range(seg - j)])

    def backward_short_group(g):
        within(g, backward_short)
        if rounds > 1:
            take(1, 1, g)

    loop(group, backward_short_group)
    for k in range(2, rounds - 1):

        def both(g):
            take(0, k, g)
            take(1, k, g)

        loop(group, both)

    def complete(c, d):
        a = [wide(decay[c, m : m + 1, :]) for m in range(modes)]
        y = []
        count = (SEGS - 1 - place if d else place).astype(jnp.float32) * (-float(seg))
        for m in range(modes):
            entering = jnp.exp(wide(rates[m : m + 1, lanes(c)]) * count)
            state = starts[d, c, m] + entering * wide(carry[d, c, m : m + 1, :])
            y.append(wide(weight[c, m : m + 1, :]) * state)
        result = [None] * seg
        order = range(seg - 1, -1, -1) if d else range(seg)
        for step, j in enumerate(order):
            if step:
                y = [y[m] * a[m] for m in range(modes)]
            result[j] = partial[d, c, j] + added(y)
        return result

    def forward_finish(c):
        conv = complete(c, 0)
        for j in range(seg):
            stream[0, c, j] = conv[j] * g32[c, pl.ds(j, SEGS, stride=seg), :]

    def forward_finish_group(g):
        if rounds > 2:
            take(0, rounds - 1, g)
        within(g, forward_finish)

    loop(group, forward_finish_group)

    def rim_copy(g):
        some = pl.ds(g * per, per)
        return pltpu.make_async_remote_copy(
            src_ref=rim_out.at[some],
            dst_ref=rim_in.at[some],
            send_sem=rim_send.at[g],
            recv_sem=rim_recv.at[g],
            device_id=(jnp.maximum(me - 1, 0), mine),
            device_id_type=pl.DeviceIdType.MESH,
        )

    def backward_finish(c):
        prod = complete(c, 1)
        for j in range(seg):
            stream[1, c, j] = prod[j] * values[c, j]
            stream[2, c, j] = prod[j] * keys[c, j]
        rim_out[c, 6:8, :] = jnp.zeros((2, LANES), jnp.float32)
        for x in range(3):
            for r in range(2):
                rim_out[c, 2 * x + r : 2 * x + r + 1, :] = stream[x, c, r, 0:1, :]

    def backward_finish_group(g):
        if rounds > 2:
            take(1, rounds - 1, g)
        within(g, backward_finish)

        @pl.when(me > 0)
        def _():
            rim_copy(g).start()

    loop(group, backward_finish_group)

    @pl.when(me == n_ctx - 1)
    def _():
        rim_in[...] = jnp.zeros(rim_in.shape, jnp.float32)

    def last_taps(c):
        for x in range(3):
            t = [wide(taps[x, j : j + 1, lanes(c)]) for j in range(3)]
            g = [stream[x, c, j] for j in range(seg)]
            for r in range(2):
                moved = pltpu.roll(g[r], SEGS - 1, 0)
                g.append(jnp.where(place == SEGS - 1, wide(rim_in[c, 2 * x + r : 2 * x + r + 1, :]), moved))
            for j in range(seg):
                placed[x, pl.ds(j, SEGS, stride=seg), :] = t[0] * g[j] + t[1] * g[j + 1] + t[2] * g[j + 2]
            out[x, :, lanes(c)] = placed[x].astype(out.dtype)

    def output_group(g):
        @pl.when(me < n_ctx - 1)
        def _():
            rim_copy(g).wait_recv()

        within(g, last_taps)

    loop(group, output_group)

    @pl.when(me < n_ctx - 1)
    def _():
        halo.wait_send()

    for d in range(2):
        for k in range(rounds):

            @pl.when(reach(d, k))
            def _():
                loop(group, lambda g: carry_copy(d, k, g).wait_send())

    @pl.when(me > 0)
    def _():
        loop(group, lambda g: rim_copy(g).wait_send())


def per_device(n_ctx, n_ch, features, grad_rows, conv_taps, decay_rate, residue, skip_gain):
    _, length, width = features.shape
    modes = decay_rate.shape[0]
    tiles = width // LANES
    seg = length // SEGS
    rounds = (n_ctx - 1).bit_length()
    group = 4 if tiles % 4 == 0 else 1
    f32 = jnp.float32
    dma = pltpu.SemaphoreType.DMA
    vmem = pl.BlockSpec(memory_space=pltpu.VMEM)
    table = pltpu.VMEM((tiles, modes, LANES), f32)
    tokens = pltpu.VMEM((tiles, seg, SEGS, LANES), f32)
    edge = pltpu.VMEM((tiles, 8, LANES), f32)
    return pl.pallas_call(
        functools.partial(kernel, n_ctx, n_ch),
        out_shape=jax.ShapeDtypeStruct(features.shape, jnp.bfloat16),
        in_specs=[pl.BlockSpec(memory_space=pl.ANY)] * 6,
        out_specs=vmem,
        scratch_shapes=[
            pltpu.VMEM(features.shape, features.dtype),
            pltpu.VMEM(conv_taps.shape, f32),
            pltpu.VMEM(decay_rate.shape, f32),
            pltpu.VMEM(residue.shape, f32),
            pltpu.VMEM((1, width), f32),
            pltpu.VMEM((3, tiles, 8 + length, LANES), f32),
            pltpu.VMEM((length, width), jnp.bfloat16),
            pltpu.VMEM((tiles, length, LANES), f32),
            table,
            table,
            table,
            table,
            pltpu.VMEM((tiles, seg, LANES), f32),
            tokens,
            tokens,
            tokens,
            pltpu.VMEM((2, tiles, modes, SEGS, LANES), f32),
            pltpu.VMEM((2, tiles, seg, SEGS, LANES), f32),
            pltpu.VMEM((2, tiles, modes, LANES), f32),
            pltpu.VMEM((2, rounds, tiles, modes, LANES), f32),
            pltpu.VMEM((2, rounds, tiles, modes, LANES), f32),
            edge,
            edge,
            pltpu.VMEM((3, tiles, seg, SEGS, LANES), f32),
            edge,
            edge,
            pltpu.VMEM((3, length, LANES), f32),
            dma((5,)),
            dma,
            dma((n_ch - 1,)),
            dma((n_ch - 1,)),
            dma,
            dma,
            dma((2, rounds, group)),
            dma((2, rounds, group)),
            dma((group,)),
            dma((group,)),
        ],
        compiler_params=pltpu.CompilerParams(
            collective_id=0, has_side_effects=True, vmem_limit_bytes=56 * 1024 * 1024
        ),
    )(features, grad_rows, conv_taps, decay_rate, residue, skip_gain[None])


def solution(mesh):
    in_specs = (
        P(None, "ctx", "ch"),
        P(("ctx", "ch"), None),
        P(None, None, "ch"),
        P(None, "ch"),
        P(None, "ch"),
        P("ch"),
    )
    body = functools.partial(per_device, mesh.shape["ctx"], mesh.shape["ch"])
    return jax.shard_map(
        body, mesh=mesh, in_specs=in_specs, out_specs=P(None, "ctx", "ch"), check_vma=False
    )
```
